128 devices in a mesh: grp: 16 (over z, y), dp: 8 (over x, core).
Axes of the slice: x: 4, y: 4, z: 4, core: 2. Of those that a mesh axis runs over, the one named last changes fastest.
Arguments:
- query_rows: bfloat16 [8, 4, 1024, 4096], P('dp', None, 'grp'), may hold values from -80 to 80
- key_rows: bfloat16 [8, 4, 1024, 1024], P('dp', None, 'grp'), may hold values from -4 to 4
- value_rows: bfloat16 [8, 4, 1024, 1024], P('dp', None, 'grp'), may hold values from -6 to 6
- segment_ids: int32 [4, 8192], replicated, may hold values from 0 to 2, never falling along the last dimension, each value on 1 to 5461 neighbouring positions
Outputs:
- attended: bfloat16 [8, 4, 1024, 4096], P('dp', None, 'grp')
The draws below stay inside these ranges and needn't reach their ends.
All inputs are finite; a program needn't handle non-finite values.
Results may differ from the reference program's by a relative error of at most 0.0039.
Values may be sent and summed in bfloat16 or wider, within the bound.
A program may use at most 64 MiB of HBM per device.

```python
import math
import jax
import jax.numpy as jnp
import numpy as np
from jax import lax

HEADS = 32
KV_HEADS = 8
HEAD_DIM = 128
DOCS = 3
GROUPS = 4
SHARD_ROWS = 1024
SEQ = 8192
N_DP = 8


def query_key_pair(key):
    first, second = jax.random.split(key)
    keyset = jnp.clip(jax.random.normal(second, (N_DP, GROUPS, SHARD_ROWS, KV_HEADS, HEAD_DIM), jnp.float32), -4.0, 4.0)
    queries = jnp.clip(jax.random.normal(first, (N_DP, GROUPS, SHARD_ROWS, HEADS, HEAD_DIM), jnp.float32), -4.0, 4.0)
    return (queries.reshape(N_DP, GROUPS, SHARD_ROWS, HEADS * HEAD_DIM), keyset.reshape(N_DP, GROUPS, SHARD_ROWS, KV_HEADS * HEAD_DIM))


def draw_query_rows(key, part):
    pair = query_key_pair(key)
    return pair[0].astype(jnp.bfloat16)


def draw_key_rows(key, part):
    pair = query_key_pair(key)
    return pair[1].astype(jnp.bfloat16)


def level_of(key, extent, cuts, low, high):
    loudness, own = 1.0, jax.random.fold_in(key, 6)
    for dim, blocks in cuts:
        heights = jnp.exp(jax.random.uniform(jax.random.fold_in(own, dim), (blocks,), jnp.float32, low / len(cuts), high / len(cuts)))
        loudness = loudness * jnp.repeat(heights, extent[dim] // blocks).reshape([-1 if axis == dim else 1 for axis in range(len(extent))])
    return loudness


def profile(amount, total, reach, slope):
    weights = [(1 << 20) // math.isqrt(standing ** slope) + 1 for standing in range(2, amount + 1)]
    surplus, counts = total - reach - (amount - 1), [1] * (amount - 1)
    while surplus > 0:
        candidates = [i for i in range(amount - 1) if counts[i] < reach]
        mass, budget = sum([weights[i] for i in candidates]), surplus
        for i in candidates:
            addition = min(reach - counts[i], max(1, budget * weights[i] // mass), surplus)
            counts[i] = counts[i] + addition
            surplus = surplus - addition
    return np.array([reach] + counts)


def ragged(rng, count, total, most, slope):
    if count == 2:
        one = jax.random.randint(rng, (), max(1, total - most), min(most, total - 1) + 1)
        return jnp.stack([one, total - one])
    sizes = jnp.asarray(profile(count, total, most, slope), jnp.int32)
    pairs = (count - 1) // 2
    giver, taker = sizes[1:1 + 2 * pairs:2], sizes[2:2 + 2 * pairs:2]
    margin = jnp.minimum(giver - 1, most - taker)
    passed = jax.random.randint(jax.random.fold_in(rng, 1), (pairs,), 0, 1 << 20) % (margin + 1)
    sizes = sizes.at[1:1 + 2 * pairs:2].set(giver - passed).at[2:2 + 2 * pairs:2].set(taker + passed)
    return sizes[jax.random.permutation(jax.random.fold_in(rng, 2), count)]


def bell_draw(key, shape, spread, limit, cuts=(), kind=jnp.bfloat16):
    entries = jax.random.normal(key, shape, jnp.float32) * spread
    if len(cuts) > 0:
        entries = level_of(key, shape, cuts, -0.22, 0.18) * entries
    return jnp.clip(entries, min=-limit, max=limit).astype(kind)


def setup_inputs(seed: int = 0) -> dict:
    arg_keys = jax.random.split(jax.random.key(seed), 5)
    query_rows = draw_query_rows(jax.random.fold_in(arg_keys[4], 71), 0)
    key_rows = draw_key_rows(jax.random.fold_in(arg_keys[4], 71), 0)
    value_rows = bell_draw(arg_keys[2], (N_DP, GROUPS, SHARD_ROWS, KV_HEADS * HEAD_DIM), 1.0, 6.0, ((0, 8), (2, 16)))
    segment_ids = jax.vmap(lambda own: jnp.searchsorted(jnp.cumsum(ragged(own, DOCS, SEQ, 2 * SEQ // 3, 2)), jnp.arange(SEQ), side="right"))(jax.random.split(arg_keys[3], GROUPS)).reshape((GROUPS, SEQ)).astype(jnp.int32)
    return dict(query_rows=query_rows, key_rows=key_rows, value_rows=value_rows, segment_ids=segment_ids)


def reference(query_rows, key_rows, value_rows, segment_ids):
    share = HEADS // KV_HEADS
    factor = 1.0 / (HEAD_DIM ** 0.5)
    position = jnp.arange(SEQ, dtype=jnp.int32)

    def one_group(group):
        queries = query_rows[:, group].reshape(SEQ, HEADS, HEAD_DIM)
        keyset = key_rows[:, group].reshape(SEQ, KV_HEADS, HEAD_DIM)
        valueset = value_rows[:, group].reshape(SEQ, KV_HEADS, HEAD_DIM)
        labels = segment_ids[group]
        allowed = (labels[:, None] == labels[None, :]) & (position[:, None] >= position[None, :])

        def one_head(head):
            shared = head // share
            scores = jnp.dot(queries[:, head], keyset[:, shared].T, preferred_element_type=jnp.float32) * factor
            scores = jnp.where(allowed, scores, -1e30)
            largest = jnp.max(scores, axis=1, keepdims=True)
            weights = jnp.where(allowed, jnp.exp(scores - largest), 0.0)
            total = jnp.sum(weights, axis=1, keepdims=True)
            rounded = weights.astype(jnp.bfloat16)
            summed = jnp.dot(rounded, valueset[:, shared], preferred_element_type=jnp.float32)
            return (summed / total).astype(jnp.bfloat16)

        heads_out = lax.map(one_head, jnp.arange(HEADS, dtype=jnp.int32))
        merged = jnp.transpose(heads_out, (1, 0, 2)).reshape(SEQ, HEADS * HEAD_DIM)
        return merged.reshape(N_DP, SHARD_ROWS, HEADS * HEAD_DIM)

    result = lax.map(one_group, jnp.arange(GROUPS, dtype=jnp.int32))
    return jnp.transpose(result, (1, 0, 2, 3))
```

```python
import functools
import math

import jax
import jax.numpy as jnp
import numpy as np
from jax import lax
from jax.experimental import pallas as pl
from jax.experimental.pallas import tpu as pltpu
from jax.sharding import PartitionSpec as P

MESH = pl.DeviceIdType.MESH
SEQ = 8192
ROWS = 64
SHARE = 4
D = 128
L = SHARE * ROWS
TILES = 32
B = 512
NPAT = B // ROWS
VR = D + 16
BIG = float(2**20)
LONGEST = 5461
FACTOR = float(np.log2(np.e) / math.sqrt(D))


def worst_steps():
    worst = 0
    for y in range(4):
        first = (4 * np.arange(TILES) + y) * ROWS
        k1 = first // B
        cuts = np.arange(1, SEQ // ROWS) * ROWS
        best = 0
        for s1 in range(1, LONGEST + 1, 32):
            for s2 in range(max(s1 + 1, SEQ - LONGEST), min(s1 + LONGEST, SEQ - 1) + 1, 32):
                start = np.where(first >= s2, s2, np.where(first >= s1, s1, 0))
                best = max(best, int((k1 - start // B + 1).sum()))
        worst = max(worst, best)
    return worst


SLOTS = 192


def where_am_i():
    gi, di = lax.axis_index("grp"), lax.axis_index("dp")
    return di // 2, gi % 4, gi // 4, di % 2


def greet(x, y, z, c, ring):
    barrier = pltpu.get_barrier_semaphore()
    n = 0
    for dx in range(4):
        for dc in range(2):
            for dz in range(4):
                if dx or dc or dz:
                    to = (((z + dz) % 4) * 4 + y, ((x + dx) % 4) * 2 + (c + dc) % 2)
                    pl.semaphore_signal(barrier, inc=1, device_id=to, device_id_type=MESH)
                    n += 1
    if ring:
        for dy in (1, 3):
            to = (z * 4 + (y + dy) % 4, x * 2 + c)
            pl.semaphore_signal(barrier, inc=1, device_id=to, device_id_type=MESH)
            n += 1
    pl.semaphore_wait(barrier, n)


def drain(ref, sem):
    pltpu.make_async_copy(ref, ref, sem).wait()


def gather_kernel(q_ref, k_ref, v_ref, qo, ko, vo, sk, sv, sq, rk, rv, rq, fk, fv, fs, hk, hv, hs):
    x, y, z, c = where_am_i()
    me = x * 2 + c
    greet(x, y, z, c, True)

    def spread(src, dst, width, send, recv):
        for dx in range(4):
            for dc in range(2):
                i = dx * 2 + dc
                for dz in range(4):
                    g, c2, z2 = (x + dx) % 4, (c + dc) % 2, (z + dz) % 4
                    cols = pl.ds(pl.multiple_of((z2 * 2 + c2) * width, 128), width)
                    if dx or dc or dz:
                        pltpu.make_async_remote_copy(
                            src_ref=src.at[0, g, :, cols],
                            dst_ref=dst,
                            send_sem=send.at[i],
                            recv_sem=recv.at[i],
                            device_id=(z2 * 4 + y, g * 2 + c2),
                            device_id_type=MESH,
                        ).start()
                    else:
                        pltpu.make_async_copy(src.at[0, g, :, cols], dst, recv.at[i]).start()

    spread(k_ref, ko.at[me, z, y], D, sk, rk)
    spread(v_ref, vo.at[me, z, y], D, sv, rv)
    spread(q_ref, qo.at[me, z], SHARE * D, sq, rq)

    up, down, far = (y + 1) % 4, (y + 3) % 4, (y + 2) % 4

    def loader(i):
        return ((x + 4 - i // 2) % 4) * 2 + (c + i % 2) % 2

    def push(ref, to, send, recv):
        pltpu.make_async_remote_copy(
            src_ref=ref,
            dst_ref=ref,
            send_sem=send,
            recv_sem=recv,
            device_id=(z * 4 + to, me),
            device_id_type=MESH,
        ).start()

    for i in range(8):
        l = loader(i)
        for buf, recv, fwd, o in ((ko, rk, fk, 0), (vo, rv, fv, 2)):
            part = buf.at[l, :, y]
            drain(part, recv.at[i])
            push(part, up, fs.at[o, i], fwd.at[0, i])
            push(part, down, fs.at[o + 1, i], fwd.at[1, i])
    for i in range(8):
        l = loader(i)
        part = ko.at[l, :, down]
        drain(part, fk.at[0, i])
        push(part, up, hs.at[0, i], hk.at[i])
        part = vo.at[l, :, up]
        drain(part, fv.at[1, i])
        push(part, down, hs.at[1, i], hv.at[i])
    for i in range(8):
        l = loader(i)
        drain(ko.at[l, :, up], fk.at[1, i])
        drain(vo.at[l, :, down], fv.at[0, i])
        drain(ko.at[l, :, far], hk.at[i])
        drain(vo.at[l, :, far], hv.at[i])
        drain(qo.at[l], rq.at[i])
        n = 4 if i else 3
        drain(ko.at[0, pl.ds(0, n), 0], sk.at[i])
        drain(vo.at[0, pl.ds(0, n), 0], sv.at[i])
        drain(qo.at[0, pl.ds(0, n)], sq.at[i])
        for o in range(4):
            drain(ko.at[0, :, 0], fs.at[o, i])
        for o in range(2):
            drain(ko.at[0, :, 0], hs.at[o, i])


def gather(q, k, v):
    dma = pltpu.SemaphoreType.DMA
    any_space = pl.BlockSpec(memory_space=pl.ANY)
    return pl.pallas_call(
        gather_kernel,
        out_shape=(
            jax.ShapeDtypeStruct((8, 4, ROWS, SHARE * D), jnp.bfloat16),
            jax.ShapeDtypeStruct((8, 4, 4, ROWS, D), jnp.bfloat16),
            jax.ShapeDtypeStruct((8, 4, 4, ROWS, D), jnp.bfloat16),
        ),
        in_specs=[any_space] * 3,
        out_specs=[any_space] * 3,
        scratch_shapes=[dma((8,))] * 6 + [dma((2, 8)), dma((2, 8)), dma((4, 8)), dma((8,)), dma((8,)), dma((2, 8))],
        compiler_params=pltpu.CompilerParams(collective_id=0, has_side_effects=True),
    )(q, k, v)


def plan_kernel(seg_ref, tab, cut):
    x, y, z, c = where_am_i()
    labels = seg_ref[pl.ds(x, 1), :]
    s1 = jnp.sum((labels == 0).astype(jnp.int32))
    s2 = s1 + jnp.sum((labels == 1).astype(jnp.int32))
    cut[0], cut[1] = s1, s2

    def tile(t, i):
        t0 = (4 * t + y) * ROWS
        start = jnp.where(t0 >= s2, s2, jnp.where(t0 >= s1, s1, 0))
        k0, k1 = start // B, t0 // B

        def one(kb, i):
            tab[0, i] = t
            tab[1, i] = kb
            tab[2, i] = (kb == k0).astype(jnp.int32)
            tab[3, i] = jnp.where(kb == k1, (t0 - kb * B) // ROWS, NPAT)
            return i + 1

        i = lax.fori_loop(k0, k1 + 1, one, i)
        tab[4, t] = i
        return i

    n = lax.fori_loop(0, TILES, tile, 0)
    cut[2] = n

    def pad(i, _):
        tab[0, i] = 0
        tab[1, i] = 0
        tab[2, i] = 1
        tab[3, i] = NPAT
        return 0

    lax.fori_loop(n, SLOTS + 8, pad, 0)


def plan(seg):
    smem = pl.BlockSpec(memory_space=pltpu.SMEM)
    return pl.pallas_call(
        plan_kernel,
        out_shape=(jax.ShapeDtypeStruct((5, SLOTS + 8), jnp.int32), jax.ShapeDtypeStruct((3,), jnp.int32)),
        in_specs=[pl.BlockSpec(memory_space=pltpu.VMEM)],
        out_specs=(smem, smem),
    )(seg)


def attend_kernel(tab, cut, q_ref, k_ref, v_ref, o_ref, qs, kd, vt, ct, sbuf, pbuf, acc, mref, mc, alr):
    x, y, z, c = where_am_i()
    s1, s2 = cut[0], cut[1]

    def transpose_values(i, _):
        s = pl.multiple_of(i * 512, 512)
        vt[0:D, pl.ds(s, 512)] = v_ref[pl.ds(s, 512), :].T
        vt[D:VR, pl.ds(s, 512)] = jnp.ones((VR - D, 512), jnp.bfloat16)
        u = s + lax.broadcasted_iota(jnp.int32, (512, D), 0)
        r = lax.broadcasted_iota(jnp.int32, (512, D), 1)
        doc = jnp.where(u >= s2, 2, jnp.where(u >= s1, 1, 0)) + ROWS
        kd[pl.ds(s, 512), :] = jnp.where(r == doc, 1.0, 0.0).astype(jnp.bfloat16)
        return 0

    lax.fori_loop(0, SEQ // 512, transpose_values, 0)

    def transpose_queries(t, _):
        s = pl.ds(pl.multiple_of(t * ROWS, ROWS), ROWS)
        tile = jnp.concatenate([q_ref[s, h * D : (h + 1) * D] for h in range(SHARE)], axis=0)
        qs[t, 0:D, :] = tile.T
        row = lax.broadcasted_iota(jnp.int32, (D, L), 1) % ROWS
        dim = lax.broadcasted_iota(jnp.int32, (D, L), 0)
        pos = (4 * t + y) * ROWS + row
        doc = jnp.where(pos >= s2, 2, jnp.where(pos >= s1, 1, 0)) + ROWS
        other = (dim >= ROWS) & (dim < ROWS + 3) & (dim != doc)
        qs[t, D : 2 * D, :] = jnp.where(dim == row, 1.0, jnp.where(other, -BIG, 0.0)).astype(jnp.bfloat16)
        return 0

    lax.fori_loop(0, TILES, transpose_queries, 0)
    u = lax.broadcasted_iota(jnp.int32, (B, D), 0)
    r = lax.broadcasted_iota(jnp.int32, (B, D), 1)
    for p in range(NPAT):
        ct[p] = jnp.where((r < ROWS) & (u > p * ROWS + r), -BIG, 0.0).astype(jnp.bfloat16)
    ct[NPAT] = jnp.zeros((B, D), jnp.bfloat16)
    acc[0] = jnp.zeros((VR, L), jnp.float32)
    mref[...] = jnp.full_like(mref, -BIG)

    def score(i, par):
        t, kb, pattern = tab[0, i], tab[1, i], tab[3, i]
        keys = pl.ds(pl.multiple_of(kb * B, B), B)
        left = jnp.concatenate([k_ref[keys, :], kd[keys, :] + ct[pattern]], axis=1)
        s = jnp.dot(left, qs[t], preferred_element_type=jnp.float32)
        sbuf[par] = s
        mc[par, 0:1, :] = jnp.max(s, axis=0, keepdims=True)

    def weigh(i, par):
        before = jnp.where(tab[2, i] == 1, -1e30, mref[0:1, :])
        top = jnp.maximum(before, mc[par, 0:1, :])
        mref[0:1, :] = top
        alr[par, 0:1, :] = jnp.exp2((before - top) * FACTOR)
        pbuf[par] = jnp.exp2(sbuf[par] * FACTOR - top * FACTOR).astype(jnp.bfloat16)

    def collect(i, par):
        keys = pl.ds(pl.multiple_of(tab[1, i] * B, B), B)
        pv = jnp.dot(vt[:, keys], pbuf[par], preferred_element_type=jnp.float32)
        acc[i + 1] = acc[i] * alr[par, 0:1, :] + pv

    score(0, 0)
    score(1, 1)
    weigh(0, 0)

    def two(j, _):
        for par in range(2):
            i = 2 * j + par
            collect(i, par)
            weigh(i + 1, 1 - par)
            score(i + 2, par)
        return 0

    lax.fori_loop(0, (cut[2] + 1) // 2, two, 0)

    def finish(t, _):
        i = tab[4, t]
        a = acc[i, 0:D, :] / acc[i, D : D + 1, :]
        at = a.T.astype(jnp.bfloat16)
        for h in range(SHARE):
            s = pl.ds(pl.multiple_of(t * ROWS, ROWS), ROWS)
            o_ref[s, h * D : (h + 1) * D] = at[h * ROWS : (h + 1) * ROWS, :]
        return 0

    lax.fori_loop(0, TILES, finish, 0)


def attend(tab, cut, q, k, v):
    smem, vmem = pl.BlockSpec(memory_space=pltpu.SMEM), pl.BlockSpec(memory_space=pltpu.VMEM)
    return pl.pallas_call(
        attend_kernel,
        out_shape=jax.ShapeDtypeStruct((TILES * ROWS, SHARE * D), jnp.bfloat16),
        in_specs=[smem, smem, vmem, vmem, vmem],
        out_specs=vmem,
        scratch_shapes=[
            pltpu.VMEM((TILES, 2 * D, L), jnp.bfloat16),
            pltpu.VMEM((SEQ, D), jnp.bfloat16),
            pltpu.VMEM((VR, SEQ), jnp.bfloat16),
            pltpu.VMEM((NPAT + 1, B, D), jnp.bfloat16),
            pltpu.VMEM((2, B, L), jnp.float32),
            pltpu.VMEM((2, B, L), jnp.bfloat16),
            pltpu.VMEM((SLOTS + 2, VR, L), jnp.float32),
            pltpu.VMEM((8, L), jnp.float32),
            pltpu.VMEM((2, 8, L), jnp.float32),
            pltpu.VMEM((2, 8, L), jnp.float32),
        ],
        compiler_params=pltpu.CompilerParams(vmem_limit_bytes=60 * 2**20),
    )(tab, cut, q.reshape(TILES * ROWS, SHARE * D), k.reshape(SEQ, D), v.reshape(SEQ, D))


def return_kernel(o_ref, out_ref, send, recv):
    x, y, z, c = where_am_i()
    greet(x, y, z, c, False)
    cols = pl.ds(pl.multiple_of((z * 2 + c) * SHARE * D, 128), SHARE * D)
    dst = out_ref.at[0, x, :, cols]
    for dx in range(4):
        for dc in range(2):
            for dz in range(4):
                l, z2 = ((x + dx) % 4) * 2 + (c + dc) % 2, (z + dz) % 4
                src = o_ref.at[l, z2]
                if dx or dc or dz:
                    pltpu.make_async_remote_copy(
                        src_ref=src,
                        dst_ref=dst,
                        send_sem=send.at[dx],
                        recv_sem=recv,
                        device_id=(z2 * 4 + y, l),
                        device_id_type=MESH,
                    ).start()
                else:
                    pltpu.make_async_copy(src, dst, recv).start()
    drain(out_ref, recv)
    for dx in range(4):
        drain(out_ref.at[0, 0, :, pl.ds(0, (8 if dx else 7) * SHARE * D)], send.at[dx])


def give_back(o):
    dma = pltpu.SemaphoreType.DMA
    any_space = pl.BlockSpec(memory_space=pl.ANY)
    return pl.pallas_call(
        return_kernel,
        out_shape=jax.ShapeDtypeStruct((1, 4, ROWS, 4096), jnp.bfloat16),
        in_specs=[any_space],
        out_specs=any_space,
        scratch_shapes=[dma((4,)), dma(())],
        compiler_params=pltpu.CompilerParams(collective_id=1, has_side_effects=True),
    )(o)


def per_device(query_rows, key_rows, value_rows, segment_ids):
    tab, cut = plan(segment_ids)
    q, k, v = gather(query_rows, key_rows, value_rows)
    out = attend(tab, cut, q, k, v)
    return give_back(out.reshape(8, 4, ROWS, SHARE * D))


def solution(mesh):
    return jax.shard_map(
        per_device,
        mesh=mesh,
        in_specs=(
            P("dp", None, "grp", None),
            P("dp", None, "grp", None),
            P("dp", None, "grp", None),
            P(),
        ),
        out_specs=P("dp", None, "grp", None),
        check_vma=False,
    )
```

```python
import math

import jax
import jax.numpy as jnp
import numpy as np
from jax import lax
from jax.experimental import pallas as pl
from jax.experimental.pallas import tpu as pltpu
from jax.sharding import PartitionSpec as P

MESH = pl.DeviceIdType.MESH
SEQ = 8192
ROWS = 64
SHARE = 4
D = 128
L = SHARE * ROWS
TILES = 32
B = 512
VR = D + 16
BIG = float(2**20)
LONGEST = 5461
FACTOR = float(np.log2(np.e) / math.sqrt(D))
BF16 = jnp.bfloat16


def phase_steps():
    worst = [0] * 4
    cuts = np.arange(0, SEQ, ROWS) + 1
    s1, s2 = np.meshgrid(cuts, cuts, indexing="ij")
    slack = LONGEST + ROWS
    fits = (s2 >= s1) & (s1 <= slack) & (s2 - s1 <= slack) & (SEQ - s2 <= slack)
    s1, s2 = s1[fits], s2[fits]
    for phase in range(4):
        zz, u = phase // 2, phase % 2
        for c in range(2):
            for low in range(2):
                count = np.zeros(s1.shape, int)
                for l in range(8):
                    t0 = l * 1024 + (c + 2 * zz) * 256 + (3 - low if u else low) * ROWS
                    start = np.where(t0 >= s2, s2, np.where(t0 >= s1, s1, 0))
                    count += t0 // B - start // B + 1
                worst[phase] = max(worst[phase], int(count.max()))
    return [n + n % 2 for n in worst]


STEPS = phase_steps()
SLOTS = max(STEPS) + 2


def drain(ref, sem):
    pltpu.make_async_copy(ref, ref, sem).wait()


def kernel(
    seg_ref, q_ref, k_ref, v_ref, out_ref, qbuf, kbuf, vbuf, qs, kd, vt, ct, sbuf, pbuf, acc, mref, mc, alr, obuf, last,
    s_kv, r_kv, s_q, r_q, s_sib, r_sib, s_par, r_par, s_hop, r_hop, s_out, r_out,
):
    gi, di = lax.axis_index("grp"), lax.axis_index("dp")
    x, y, z, c = di // 2, gi % 4, gi // 4, di % 2
    half = y // 2
    low = jnp.minimum(y, 3 - y)
    up = (y > 1).astype(jnp.int32)
    mate = y + 1 - 2 * (y % 2)
    core = z % 2
    mine = core == c
    sibling = (gi, x * 2 + 1 - c)
    partner = (z * 4 + mate, di)

    barrier = pltpu.get_barrier_semaphore()
    n = 0
    for dx in range(4):
        for dz in range(4):
            for dh in range(2):
                for dc in range(2):
                    if dx or dz or dh or dc:
                        to = (((z + dz) % 4) * 4 + (3 - y if dh else y), ((x + dx) % 4) * 2 + (c + dc) % 2)
                        pl.semaphore_signal(barrier, inc=1, device_id=to, device_id_type=MESH)
                        n += 1
    pl.semaphore_signal(barrier, inc=1, device_id=partner, device_id_type=MESH)
    pl.semaphore_wait(barrier, n + 1)

    def remote(src, dst, send, recv, to):
        pltpu.make_async_remote_copy(
            src_ref=src, dst_ref=dst, send_sem=send, recv_sem=recv, device_id=to, device_id_type=MESH
        ).start()

    def spread(pairs, width, send, recv):
        for dx in range(4):
            for dz in range(4):
                for dh in range(2):
                    g, z2 = (x + dx) % 4, (z + dz) % 4
                    h2, y2 = (1 - half, 3 - y) if dh else (half, y)
                    cols = pl.ds(pl.multiple_of((z2 * 2 + h2) * width, 128), width)
                    to = (z2 * 4 + y2, g * 2 + core)
                    for src, dst in pairs:
                        piece = src.at[0, g, :, cols]
                        if dx or dz or dh:
                            remote(piece, dst, send.at[dx], recv.at[di], to)
                        else:

                            @pl.when(mine)
                            def _():
                                pltpu.make_async_copy(piece, dst, recv.at[di]).start()

                            @pl.when(jnp.logical_not(mine))
                            def _():
                                remote(piece, dst, send.at[dx], recv.at[di], to)

    here = (di * 2 + z // 2, core, low, up)
    spread(((k_ref, kbuf.at[here]), (v_ref, vbuf.at[here])), D, s_kv, r_kv)
    spread(((q_ref, qbuf.at[di, z // 2, up]),), SHARE * D, s_q, r_q)

    labels = seg_ref[pl.ds(x, 1), :]
    s1 = jnp.sum((labels == 0).astype(jnp.int32))
    s2 = s1 + jnp.sum((labels == 1).astype(jnp.int32))

    def document(pos):
        return jnp.where(pos >= s2, 2, jnp.where(pos >= s1, 1, 0))

    u = lax.broadcasted_iota(jnp.int32, (B, D), 0)
    r = lax.broadcasted_iota(jnp.int32, (B, D), 1)
    slot = (u // ROWS) % 4
    place = (u // 256) * 256 + u % ROWS + jnp.where(slot % 2 == 1, 3 - slot // 2, slot // 2) * ROWS

    def key_documents(kb, _):
        kd[kb] = jnp.where(r == document(place + kb * B) + ROWS, 1.0, 0.0).astype(BF16)
        vt[kb, D:VR, :] = jnp.ones((VR - D, B), BF16)
        return 0

    lax.fori_loop(0, SEQ // B, key_documents, 0)
    for side in range(2):
        mine_y = 3 - low if side else low
        ct[side] = jnp.where((r < ROWS) & (place > c * 256 + mine_y * ROWS + r), -BIG, 0.0).astype(BF16)
    ct[2] = jnp.zeros((B, D), BF16)
    row = lax.broadcasted_iota(jnp.int32, (D, L), 1) % ROWS
    dim = lax.broadcasted_iota(jnp.int32, (D, L), 0)

    def block_start(l, zz, side):
        return l * 1024 + (c + 2 * zz) * 256 + (3 - low if side else low) * ROWS

    def query_documents(l, _):
        for zz in range(2):
            for side in range(2):
                doc = document(block_start(l, zz, side) + row) + ROWS
                other = (dim >= ROWS) & (dim < ROWS + 3) & (dim != doc)
                value = jnp.where(dim == row, 1.0, jnp.where(other, -BIG, 0.0))
                qs[(l * 2 + zz) * 2 + side, D : 2 * D, :] = value.astype(BF16)
        return 0

    lax.fori_loop(0, 8, query_documents, 0)
    acc[0] = jnp.zeros((VR, L), jnp.float32)
    mref[...] = jnp.full_like(mref, -BIG)

    def loader(i):
        return ((x + 4 - i // 2) % 4) * 2 + (c + i % 2) % 2

    for i in range(8):
        l = loader(i)
        drain(kbuf.at[0], r_kv.at[l])
        for buf in (kbuf, vbuf):
            part = buf.at[pl.ds(2 * l, 2), c, low]
            remote(part, part, s_sib.at[i], r_sib.at[l], sibling)
            remote(part, part, s_par.at[i], r_par.at[l], partner)
    theirs = jnp.minimum(mate, 3 - mate)
    for i in range(8):
        l = loader(i)
        drain(kbuf.at[0], r_par.at[l])
        for buf in (kbuf, vbuf):
            part = buf.at[pl.ds(2 * l, 2), c, theirs]
            remote(part, part, s_hop.at[i], r_hop.at[l], sibling)

    def turn_queries(l, _):
        drain(qbuf.at[0], r_q.at[l])
        for zz in range(2):
            for side in range(2):
                t = (l * 2 + zz) * 2 + side
                tile = jnp.concatenate([qbuf[l, zz, side, :, h * D : (h + 1) * D] for h in range(SHARE)], axis=0)
                qs[t, 0:D, :] = tile.T
        return 0

    lax.fori_loop(0, 8, turn_queries, 0)

    def turn_values(l, _):
        drain(kbuf.at[0], r_sib.at[l])
        drain(kbuf.at[0], r_hop.at[l])
        for zz in range(2):
            vt[2 * l + zz, 0:D, :] = vbuf[2 * l + zz].reshape(B, D).T
        return 0

    lax.fori_loop(0, 8, turn_values, 0)

    head = z * 2 + half
    result = out_ref.at[0, x, :, pl.ds(pl.multiple_of(head * SHARE * D, 128), SHARE * D)]

    for phase in range(4):
        zz, side = phase // 2, phase % 2

        def first_block(l):
            t0 = block_start(l, zz, side)
            return jnp.where(t0 >= s2, s2, jnp.where(t0 >= s1, s1, 0)) // B

        def advance(l, kb):
            done = kb >= 2 * l + zz
            l2 = jnp.where(done, jnp.minimum(l + 1, 7), l)
            return l2, jnp.where(done, first_block(l2), kb + 1)

        def score(l, kb, par):
            mask = ct[jnp.where(kb == 2 * l + zz, side, 2)]
            left = jnp.concatenate([kbuf[kb].reshape(B, D), kd[kb] + mask], axis=1)
            s = jnp.dot(left, qs[(l * 2 + zz) * 2 + side], preferred_element_type=jnp.float32)
            sbuf[par] = s
            mc[par, 0:1, :] = jnp.max(s, axis=0, keepdims=True)

        def weigh(first, par):
            before = jnp.where(first == 1, -1e30, mref[0:1, :])
            top = jnp.maximum(before, mc[par, 0:1, :])
            mref[0:1, :] = top
            alr[par, 0:1, :] = jnp.exp2((before - top) * FACTOR)
            pbuf[par] = jnp.exp2(sbuf[par] * FACTOR - top * FACTOR).astype(BF16)

        def collect(i, kb, par):
            pv = jnp.dot(vt[kb], pbuf[par], preferred_element_type=jnp.float32)
            acc[i + 1] = acc[i] * alr[par, 0:1, :] + pv

        def opens(l, kb):
            return (kb == first_block(l)).astype(jnp.int32)

        l0 = jnp.int32(0)
        b0 = first_block(l0)
        l1, b1 = advance(l0, b0)
        score(l0, b0, 0)
        score(l1, b1, 1)
        weigh(jnp.int32(1), 0)

        def two(j, carry):
            b0, b1, f1, l1 = carry
            for par in range(2):
                collect(2 * j + par, b0, par)
                weigh(f1, 1 - par)
                l2, b2 = advance(l1, b1)
                score(l2, b2, par)
                b0, b1, f1, l1 = b1, b2, opens(l2, b2), l2
            return b0, b1, f1, l1

        lax.fori_loop(0, STEPS[phase] // 2, two, (b0, b1, opens(l1, b1), l1))

        def count(l, done):
            done = done + 2 * l + zz - first_block(l) + 1
            last[l] = jnp.minimum(done, STEPS[phase])
            return done

        lax.fori_loop(0, 8, count, jnp.int32(0))

        def finish(j, _):
            l = (di + j) % 8
            i = last[l]
            a = acc[i, 0:D, :] / acc[i, D : D + 1, :]
            at = a.T.astype(BF16)
            tile = obuf.at[l, zz, side]
            for h in range(SHARE):
                obuf[l, zz, side, :, h * D : (h + 1) * D] = at[h * ROWS : (h + 1) * ROWS, :]
            to_z, to_y = c + 2 * zz, 3 - low if side else low
            own = (l == di) & (to_z == z) & (to_y == y)

            @pl.when(own)
            def _():
                pltpu.make_async_copy(tile, result, r_out).start()

            @pl.when(jnp.logical_not(own))
            def _():
                remote(tile, result, s_out.at[l, phase], r_out, (to_z * 4 + to_y, l))

            return 0

        lax.fori_loop(0, 8, finish, 0)

    drain(out_ref, r_out)
    for dx in range(4):
        if dx:
            drain(kbuf.at[pl.ds(0, 2)], s_kv.at[dx])
            drain(qbuf.at[pl.ds(0, 2)], s_q.at[dx])
        else:

            @pl.when(mine)
            def _():
                drain(kbuf.at[pl.ds(0, 7), :, 0, 0], s_kv.at[dx])
                drain(qbuf.at[pl.ds(0, 7), 0, 0], s_q.at[dx])

            @pl.when(jnp.logical_not(mine))
            def _():
                drain(kbuf.at[pl.ds(0, 2)], s_kv.at[dx])
                drain(qbuf.at[pl.ds(0, 2)], s_q.at[dx])

    def sent(i, _):
        for sem in (s_sib, s_par, s_hop):
            drain(kbuf.at[0], sem.at[i])
        for phase in range(4):
            zz, side = phase // 2, phase % 2
            to_z, to_y = c + 2 * zz, 3 - low if side else low

            @pl.when(jnp.logical_not((i == di) & (to_z == z) & (to_y == y)))
            def _():
                drain(obuf.at[0, 0, 0], s_out.at[i, phase])

        return 0

    lax.fori_loop(0, 8, sent, 0)


def per_device(query_rows, key_rows, value_rows, segment_ids):
    dma = pltpu.SemaphoreType.DMA
    vmem = pltpu.VMEM
    any_space = pl.BlockSpec(memory_space=pl.ANY)
    return pl.pallas_call(
        kernel,
        out_shape=jax.ShapeDtypeStruct((1, 4, ROWS, 4096), BF16),
        in_specs=[pl.BlockSpec(memory_space=vmem)] + [any_space] * 3,
        out_specs=any_space,
        scratch_shapes=[
            vmem((8, 2, 2, ROWS, SHARE * D), BF16),
            vmem((16, 2, 2, 2, ROWS, D), BF16),
            vmem((16, 2, 2, 2, ROWS, D), BF16),
            vmem((TILES, 2 * D, L), BF16),
            vmem((16, B, D), BF16),
            vmem((16, VR, B), BF16),
            vmem((3, B, D), BF16),
            vmem((2, B, L), jnp.float32),
            vmem((2, B, L), BF16),
            vmem((SLOTS, VR, L), jnp.float32),
            vmem((8, L), jnp.float32),
            vmem((2, 8, L), jnp.float32),
            vmem((2, 8, L), jnp.float32),
            vmem((8, 2, 2, ROWS, SHARE * D), BF16),
            pltpu.SMEM((8,), jnp.int32),
            dma((4,)), dma((8,)), dma((4,)), dma((8,)), dma((8,)), dma((8,)),
            dma((8,)), dma((8,)), dma((8,)), dma((8,)), dma((8, 4)), dma(()),
        ],
        compiler_params=pltpu.CompilerParams(
            collective_id=0, has_side_effects=True, vmem_limit_bytes=60 * 2**20
        ),
    )(segment_ids, query_rows, key_rows, value_rows)


def solution(mesh):
    return jax.shard_map(
        per_device,
        mesh=mesh,
        in_specs=(
            P("dp", None, "grp", None),
            P("dp", None, "grp", None),
            P("dp", None, "grp", None),
            P(),
        ),
        out_specs=P("dp", None, "grp", None),
        check_vma=False,
    )
```

```python
import math

import jax
import jax.numpy as jnp
import numpy as np
from jax import lax
from jax.experimental import pallas as pl
from jax.experimental.pallas import tpu as pltpu
from jax.sharding import PartitionSpec as P

MESH = pl.DeviceIdType.MESH
SEQ = 8192
ROWS = 64
SHARE = 4
D = 128
L = SHARE * ROWS
TILES = 32
B = 512
VR = D + 16
BIG = float(2**20)
LONGEST = 5461
FACTOR = float(np.log2(np.e) / math.sqrt(D))
BF16 = jnp.bfloat16


def phase_steps():
    worst = [0] * 2
    cuts = np.arange(0, SEQ, ROWS) + 1
    s1, s2 = np.meshgrid(cuts, cuts, indexing="ij")
    slack = LONGEST + ROWS
    fits = (s2 >= s1) & (s1 <= slack) & (s2 - s1 <= slack) & (SEQ - s2 <= slack)
    s1, s2 = s1[fits], s2[fits]
    for zz in range(2):
        for c in range(2):
            for y in range(4):
                count = np.zeros(s1.shape, int)
                for l in range(8):
                    t0 = l * 1024 + (c + 2 * zz) * 256 + y * ROWS
                    start = np.where(t0 >= s2, s2, np.where(t0 >= s1, s1, 0))
                    count += t0 // B - start // B + 1
                worst[zz] = max(worst[zz], int(count.max()))
    return [n + n % 2 for n in worst]


STEPS = phase_steps()
SLOTS = max(STEPS) + 2


def drain(ref, sem):
    pltpu.make_async_copy(ref, ref, sem).wait()


def kernel(
    seg_ref, q_ref, k_ref, v_ref, out_ref, qbuf, kva, kvb, qs, qd, kd, vt, ct, sbuf, pbuf, acc, mref, mc, alr, obuf, last,
    s_kv, r_kv, s_q, r_q, s_f, r_f, s_r, r_r, r_s, s_out, r_out,
):
    gi, di = lax.axis_index("grp"), lax.axis_index("dp")
    x, y, z, c = di // 2, gi % 4, gi // 4, di % 2
    core = z % 2
    mine = core == c
    other_core = (gi, x * 2 + 1 - c)
    up, down, far = (y + 1) % 4, (y + 3) % 4, (y + 2) % 4
    up_chip, down_chip = (z * 4 + up, di), (z * 4 + down, di)
    kvs = (kva, kvb)

    barrier = pltpu.get_barrier_semaphore()
    n = 0
    for dx in range(4):
        for dz in range(4):
            for dc in range(2):
                if dx or dz or dc:
                    to = (((z + dz) % 4) * 4 + y, ((x + dx) % 4) * 2 + (c + dc) % 2)
                    pl.semaphore_signal(barrier, inc=1, device_id=to, device_id_type=MESH)
                    n += 1
    for to in (up_chip, down_chip):
        pl.semaphore_signal(barrier, inc=1, device_id=to, device_id_type=MESH)
        n += 1
    pl.semaphore_wait(barrier, n)

    def remote(src, dst, send, recv, to):
        pltpu.make_async_remote_copy(
            src_ref=src, dst_ref=dst, send_sem=send, recv_sem=recv, device_id=to, device_id_type=MESH
        ).start()

    def spread(pairs, h, width, send, recv):
        for dx in range(4):
            for dz in range(4):
                g, z2 = (x + dx) % 4, (z + dz) % 4
                cols = pl.ds(pl.multiple_of((z2 * 2 + h) * width, 128), width)
                to = (z2 * 4 + y, g * 2 + core)
                for src, dst in pairs:
                    piece = src.at[0, g, :, cols]
                    if dx or dz:
                        remote(piece, dst, send.at[h, dx], recv.at[h, x], to)
                    else:

                        @pl.when(mine)
                        def _():
                            pltpu.make_async_copy(piece, dst, recv.at[h, x]).start()

                        @pl.when(jnp.logical_not(mine))
                        def _():
                            remote(piece, dst, send.at[h, dx], recv.at[h, x], to)

    def spread_head(h):
        block = di * 2 + z // 2
        spread(((k_ref, kvs[h].at[block, core, y, 0]), (v_ref, kvs[h].at[block, core, y, 1])), h, D, s_kv, r_kv)
        spread(((q_ref, qbuf.at[h, di, z // 2]),), h, SHARE * D, s_q, r_q)

    whole, part_of_one = kva.at[0, 0], kva.at[0, 0, :, 0]

    def source(i):
        return (x + 4 - i) % 4

    def part(h, xs, whose):
        return kvs[h].at[pl.ds(4 * xs, 4), c, whose]

    def forward(h):
        for i in range(4):
            xs = source(i)
            drain(whole, r_kv.at[h, xs])
            own = part(h, xs, y)
            remote(own, own, s_f.at[h, 0, i], r_f.at[h, 0, xs], up_chip)
            remote(own, own, s_f.at[h, 1, i], r_f.at[h, 1, xs], down_chip)
            remote(own, own, s_f.at[h, 2, i], r_s.at[h, 0, xs], other_core)

    def relay(h):
        for i in range(4):
            xs = source(i)
            drain(whole, r_f.at[h, 0, xs])
            keys = kvs[h].at[pl.ds(4 * xs, 4), c, down, 0]
            remote(keys, keys, s_r.at[h, 0, i], r_r.at[h, 0, xs], up_chip)
            drain(whole, r_f.at[h, 1, xs])
            values = kvs[h].at[pl.ds(4 * xs, 4), c, up, 1]
            remote(values, values, s_r.at[h, 1, i], r_r.at[h, 1, xs], down_chip)
            remote(part(h, xs, down), part(h, xs, down), s_r.at[h, 2, i], r_s.at[h, 1, xs], other_core)
            remote(part(h, xs, up), part(h, xs, up), s_r.at[h, 3, i], r_s.at[h, 2, xs], other_core)

    def complete(h):
        for i in range(4):
            xs = source(i)
            drain(part_of_one, r_r.at[h, 0, xs])
            drain(part_of_one, r_r.at[h, 1, xs])
            remote(part(h, xs, far), part(h, xs, far), s_r.at[h, 4, i], r_s.at[h, 3, xs], other_core)

    spread_head(0)

    labels = seg_ref[pl.ds(x, 1), :]
    s1 = jnp.sum((labels == 0).astype(jnp.int32))
    s2 = s1 + jnp.sum((labels == 1).astype(jnp.int32))

    def document(pos):
        return jnp.where(pos >= s2, 2, jnp.where(pos >= s1, 1, 0))

    u = lax.broadcasted_iota(jnp.int32, (B, D), 0)
    r = lax.broadcasted_iota(jnp.int32, (B, D), 1)

    def key_documents(kb, _):
        kd[kb] = jnp.where(r == document(u + kb * B) + ROWS, 1.0, 0.0).astype(BF16)
        vt[kb, D:VR, :] = jnp.ones((VR - D, B), BF16)
        return 0

    lax.fori_loop(0, SEQ // B, key_documents, 0)
    ct[0] = jnp.where((r < ROWS) & (u > c * 256 + y * ROWS + r), -BIG, 0.0).astype(BF16)
    ct[1] = jnp.zeros((B, D), BF16)
    row = lax.broadcasted_iota(jnp.int32, (D, L), 1) % ROWS
    dim = lax.broadcasted_iota(jnp.int32, (D, L), 0)

    def query_documents(kb, _):
        doc = document(kb * B + c * 256 + y * ROWS + row) + ROWS
        other = (dim >= ROWS) & (dim < ROWS + 3) & (dim != doc)
        qd[kb] = jnp.where(dim == row, 1.0, jnp.where(other, -BIG, 0.0)).astype(BF16)
        return 0

    lax.fori_loop(0, SEQ // B, query_documents, 0)
    acc[0] = jnp.zeros((VR, L), jnp.float32)
    mref[...] = jnp.full_like(mref, -BIG)

    def prepare(h):
        def turn_queries(xs, _):
            drain(qbuf.at[0, pl.ds(0, 2)], r_q.at[h, xs])
            for t in range(4):
                l, zz = 2 * xs + t // 2, t % 2
                tile = jnp.concatenate([qbuf[h, l, zz, :, j * D : (j + 1) * D] for j in range(SHARE)], axis=0)
                qs[h * 16 + 4 * xs + t] = tile.T
            return 0

        lax.fori_loop(0, 4, turn_queries, 0)

        def turn_values(xs, _):
            for o in range(4):
                drain(whole, r_s.at[h, o, xs])
            for t in range(4):
                vt[4 * xs + t, 0:D, :] = kvs[h][4 * xs + t, :, :, 1].reshape(B, D).T
            return 0

        lax.fori_loop(0, 4, turn_values, 0)

    def work(h, zz, between):
        kv = kvs[h]

        def first_block(l):
            t0 = l * 1024 + (c + 2 * zz) * 256 + y * ROWS
            return jnp.where(t0 >= s2, s2, jnp.where(t0 >= s1, s1, 0)) // B

        def advance(l, kb):
            done = kb >= 2 * l + zz
            l2 = jnp.where(done, jnp.minimum(l + 1, 7), l)
            return l2, jnp.where(done, first_block(l2), kb + 1)

        def score(l, kb, par):
            mask = ct[jnp.where(kb == 2 * l + zz, 0, 1)]
            left = jnp.concatenate([kv[kb, :, :, 0].reshape(B, D), kd[kb] + mask], axis=1)
            right = jnp.concatenate([qs[h * 16 + 2 * l + zz], qd[2 * l + zz]], axis=0)
            s = jnp.dot(left, right, preferred_element_type=jnp.float32)
            sbuf[par] = s
            mc[par, 0:1, :] = jnp.max(s, axis=0, keepdims=True)

        def weigh(first, par):
            before = jnp.where(first == 1, -1e30, mref[0:1, :])
            top = jnp.maximum(before, mc[par, 0:1, :])
            mref[0:1, :] = top
            alr[par, 0:1, :] = jnp.exp2((before - top) * FACTOR)
            pbuf[par] = jnp.exp2(sbuf[par] * FACTOR - top * FACTOR).astype(BF16)

        def collect(i, kb, par):
            pv = jnp.dot(vt[kb], pbuf[par], preferred_element_type=jnp.float32)
            acc[i + 1] = acc[i] * alr[par, 0:1, :] + pv

        def opens(l, kb):
            return (kb == first_block(l)).astype(jnp.int32)

        l0 = jnp.int32(0)
        b0 = first_block(l0)
        l1, b1 = advance(l0, b0)
        score(l0, b0, 0)
        score(l1, b1, 1)
        weigh(jnp.int32(1), 0)

        def two(j, carry):
            b0, b1, f1, l1 = carry
            for par in range(2):
                collect(2 * j + par, b0, par)
                weigh(f1, 1 - par)
                l2, b2 = advance(l1, b1)
                score(l2, b2, par)
                b0, b1, f1, l1 = b1, b2, opens(l2, b2), l2
            return b0, b1, f1, l1

        carry = (b0, b1, opens(l1, b1), l1)
        pairs = STEPS[zz] // 2
        if between is None:
            lax.fori_loop(0, pairs, two, carry)
        else:
            carry = lax.fori_loop(0, pairs // 2, two, carry)
            between(h + 1)
            lax.fori_loop(pairs // 2, pairs, two, carry)

        def count(l, done):
            done = done + 2 * l + zz - first_block(l) + 1
            last[l] = jnp.minimum(done, STEPS[zz])
            return done

        lax.fori_loop(0, 8, count, jnp.int32(0))
        to_z = c + 2 * zz
        cols = pl.ds(pl.multiple_of((z * 2 + h) * SHARE * D, 128), SHARE * D)

        def finish(j, _):
            l = (di + j) % 8
            i = last[l]
            a = acc[i, 0:D, :] / acc[i, D : D + 1, :]
            at = a.T.astype(BF16)
            tile = obuf.at[h, l, zz]
            for o in range(SHARE):
                obuf[h, l, zz, :, o * D : (o + 1) * D] = at[o * ROWS : (o + 1) * ROWS, :]
            own = (l == di) & (to_z == z)
            result = out_ref.at[0, x, :, cols]

            @pl.when(own)
            def _():
                pltpu.make_async_copy(tile, result, r_out).start()

            @pl.when(jnp.logical_not(own))
            def _():
                remote(tile, result, s_out.at[h, zz, l], r_out, (to_z * 4 + y, l))

            return 0

        lax.fori_loop(0, 8, finish, 0)

    forward(0)
    spread_head(1)
    relay(0)
    complete(0)
    prepare(0)
    work(0, 0, forward)
    relay(1)
    work(0, 1, complete)
    prepare(1)
    work(1, 0, None)
    work(1, 1, None)

    drain(out_ref, r_out)
    for h in range(2):
        for dx in range(4):
            if dx:
                drain(whole, s_kv.at[h, dx])
                drain(qbuf.at[0, pl.ds(0, 2)], s_q.at[h, dx])
            else:

                @pl.when(mine)
                def _():
                    drain(kva.at[0, 0, pl.ds(0, 3)], s_kv.at[h, dx])
                    drain(qbuf.at[0, pl.ds(0, 3), 0], s_q.at[h, dx])

                @pl.when(jnp.logical_not(mine))
                def _():
                    drain(whole, s_kv.at[h, dx])
                    drain(qbuf.at[0, pl.ds(0, 2)], s_q.at[h, dx])

    def sent(i, _):
        for h in range(2):
            for o in range(3):
                drain(whole, s_f.at[h, o, i])
            for o in range(5):
                drain(whole if o > 1 else part_of_one, s_r.at[h, o, i])
        return 0

    lax.fori_loop(0, 4, sent, 0)

    def returned(l, _):
        for h in range(2):
            for zz in range(2):

                @pl.when(jnp.logical_not((l == di) & (c + 2 * zz == z)))
                def _():
                    drain(obuf.at[0, 0, 0], s_out.at[h, zz, l])

        return 0

    lax.fori_loop(0, 8, returned, 0)


def per_device(query_rows, key_rows, value_rows, segment_ids):
    dma = pltpu.SemaphoreType.DMA
    vmem = pltpu.VMEM
    any_space = pl.BlockSpec(memory_space=pl.ANY)
    return pl.pallas_call(
        kernel,
        out_shape=jax.ShapeDtypeStruct((1, 4, ROWS, 4096), BF16),
        in_specs=[pl.BlockSpec(memory_space=vmem)] + [any_space] * 3,
        out_specs=any_space,
        scratch_shapes=[
            vmem((2, 8, 2, ROWS, SHARE * D), BF16),
            vmem((16, 2, 4, 2, ROWS, D), BF16),
            vmem((16, 2, 4, 2, ROWS, D), BF16),
            vmem((TILES, D, L), BF16),
            vmem((16, D, L), BF16),
            vmem((16, B, D), BF16),
            vmem((16, VR, B), BF16),
            vmem((2, B, D), BF16),
            vmem((2, B, L), jnp.float32),
            vmem((2, B, L), BF16),
            vmem((SLOTS, VR, L), jnp.float32),
            vmem((8, L), jnp.float32),
            vmem((2, 8, L), jnp.float32),
            vmem((2, 8, L), jnp.float32),
            vmem((2, 8, 2, ROWS, SHARE * D), BF16),
            pltpu.SMEM((8,), jnp.int32),
            dma((2, 4)), dma((2, 4)), dma((2, 4)), dma((2, 4)), dma((2, 3, 4)), dma((2, 2, 4)),
            dma((2, 5, 4)), dma((2, 2, 4)), dma((2, 4, 4)), dma((2, 2, 8)), dma(()),
        ],
        compiler_params=pltpu.CompilerParams(
            collective_id=0, has_side_effects=True, vmem_limit_bytes=60 * 2**20
        ),
    )(segment_ids, query_rows, key_rows, value_rows)


def solution(mesh):
    return jax.shard_map(
        per_device,
        mesh=mesh,
        in_specs=(
            P("dp", None, "grp", None),
            P("dp", None, "grp", None),
            P("dp", None, "grp", None),
            P(),
        ),
        out_specs=P("dp", None, "grp", None),
        check_vma=False,
    )
```

```python
import math

import jax
import jax.numpy as jnp
import numpy as np
from jax import lax
from jax.experimental import pallas as pl
from jax.experimental.pallas import tpu as pltpu
from jax.sharding import PartitionSpec as P

MESH = pl.DeviceIdType.MESH
SEQ = 8192
ROWS = 64
SHARE = 4
D = 128
L = SHARE * ROWS
TILES = 32
B = 512
VR = D + 16
BIG = float(2**20)
LONGEST = 5461
FACTOR = float(np.log2(np.e) / math.sqrt(D))
BF16 = jnp.bfloat16


def phase_steps():
    worst = [0] * 2
    cuts = np.arange(0, SEQ, ROWS) + 1
    s1, s2 = np.meshgrid(cuts, cuts, indexing="ij")
    slack = LONGEST + ROWS
    fits = (s2 >= s1) & (s1 <= slack) & (s2 - s1 <= slack) & (SEQ - s2 <= slack)
    s1, s2 = s1[fits], s2[fits]
    for zz in range(2):
        for c in range(2):
            for y in range(4):
                count = np.zeros(s1.shape, int)
                for l in range(8):
                    t0 = l * 1024 + (c + 2 * zz) * 256 + y * ROWS
                    start = np.where(t0 >= s2, s2, np.where(t0 >= s1, s1, 0))
                    count += t0 // B - start // B + 1
                worst[zz] = max(worst[zz], int(count.max()))
    return [n + n % 2 for n in worst]


STEPS = phase_steps()
SLOTS = max(STEPS) + 2


def drain(ref, sem):
    pltpu.make_async_copy(ref, ref, sem).wait()


def kernel(
    seg_ref, q_ref, k_ref, v_ref, out_ref, qbuf, kva, kvb, qs, qd, kd, vt, ct, sbuf, pbuf, acc, mref, mc, alr, obuf, last,
    s_kv, r_kv, s_q, r_q, s_f, r_f, s_r, r_r, r_s, s_out, r_out,
):
    gi, di = lax.axis_index("grp"), lax.axis_index("dp")
    x, y, z, c = di // 2, gi % 4, gi // 4, di % 2
    core = z % 2
    mine = core == c
    other_core = (gi, x * 2 + 1 - c)
    up, down, far = (y + 1) % 4, (y + 3) % 4, (y + 2) % 4
    up_chip, down_chip = (z * 4 + up, di), (z * 4 + down, di)
    kvs = (kva, kvb)

    barrier = pltpu.get_barrier_semaphore()
    n = 0
    for dx in range(4):
        for dz in range(4):
            for dc in range(2):
                if dx or dz or dc:
                    to = (((z + dz) % 4) * 4 + y, ((x + dx) % 4) * 2 + (c + dc) % 2)
                    pl.semaphore_signal(barrier, inc=1, device_id=to, device_id_type=MESH)
                    n += 1
    for to in (up_chip, down_chip):
        pl.semaphore_signal(barrier, inc=1, device_id=to, device_id_type=MESH)
        n += 1
    pl.semaphore_wait(barrier, n)

    def remote(src, dst, send, recv, to):
        pltpu.make_async_remote_copy(
            src_ref=src, dst_ref=dst, send_sem=send, recv_sem=recv, device_id=to, device_id_type=MESH
        ).start()

    def spread(pairs, h, width, send, recv):
        for dx in range(4):
            for dz in range(4):
                g, z2 = (x + dx) % 4, (z + dz) % 4
                cols = pl.ds(pl.multiple_of((z2 * 2 + h) * width, 128), width)
                to = (z2 * 4 + y, g * 2 + core)
                for src, dst in pairs:
                    piece = src.at[0, g, :, cols]
                    if dx or dz:
                        remote(piece, dst, send.at[h, dx], recv.at[h, x], to)
                    else:

                        @pl.when(mine)
                        def _():
                            pltpu.make_async_copy(piece, dst, recv.at[h, x]).start()

                        @pl.when(jnp.logical_not(mine))
                        def _():
                            remote(piece, dst, send.at[h, dx], recv.at[h, x], to)

    def spread_head(h):
        block = di * 2 + z // 2
        spread(((k_ref, kvs[h].at[block, core, y, 0]), (v_ref, kvs[h].at[block, core, y, 1])), h, D, s_kv, r_kv)
        spread(((q_ref, qbuf.at[h, di, z // 2]),), h, SHARE * D, s_q, r_q)

    whole, part_of_one = kva.at[0, 0], kva.at[0, 0, :, 0]

    def source(i):
        return (x + 4 - i) % 4

    def part(h, xs, whose):
        return kvs[h].at[pl.ds(4 * xs, 4), c, whose]

    def forward(h):
        for i in range(4):
            xs = source(i)
            drain(whole, r_kv.at[h, xs])
            own = part(h, xs, y)
            remote(own, own, s_f.at[h, 0, i], r_f.at[h, 0, xs], up_chip)
            remote(own, own, s_f.at[h, 1, i], r_f.at[h, 1, xs], down_chip)
            remote(own, own, s_f.at[h, 2, i], r_s.at[h, 0, xs], other_core)

    def relay(h):
        for i in range(4):
            xs = source(i)
            drain(whole, r_f.at[h, 0, xs])
            keys = kvs[h].at[pl.ds(4 * xs, 4), c, down, 0]
            remote(keys, keys, s_r.at[h, 0, i], r_r.at[h, 0, xs], up_chip)
            drain(whole, r_f.at[h, 1, xs])
            values = kvs[h].at[pl.ds(4 * xs, 4), c, up, 1]
            remote(values, values, s_r.at[h, 1, i], r_r.at[h, 1, xs], down_chip)
            remote(part(h, xs, down), part(h, xs, down), s_r.at[h, 2, i], r_s.at[h, 1, xs], other_core)
            remote(part(h, xs, up), part(h, xs, up), s_r.at[h, 3, i], r_s.at[h, 2, xs], other_core)

    def complete(h):
        for i in range(4):
            xs = source(i)
            drain(part_of_one, r_r.at[h, 0, xs])
            drain(part_of_one, r_r.at[h, 1, xs])
            remote(part(h, xs, far), part(h, xs, far), s_r.at[h, 4, i], r_s.at[h, 3, xs], other_core)

    spread_head(0)

    labels = seg_ref[pl.ds(x, 1), :]
    s1 = jnp.sum((labels == 0).astype(jnp.int32))
    s2 = s1 + jnp.sum((labels == 1).astype(jnp.int32))

    def document(pos):
        return jnp.where(pos >= s2, 2, jnp.where(pos >= s1, 1, 0))

    u = lax.broadcasted_iota(jnp.int32, (B, D), 0)
    r = lax.broadcasted_iota(jnp.int32, (B, D), 1)

    def key_documents(kb, _):
        kd[kb] = jnp.where(r == document(u + kb * B) + ROWS, 1.0, 0.0).astype(BF16)
        vt[kb, D:VR, :] = jnp.ones((VR - D, B), BF16)
        return 0

    lax.fori_loop(0, SEQ // B, key_documents, 0)
    ct[0] = jnp.where((r < ROWS) & (u > c * 256 + y * ROWS + r), -BIG, 0.0).astype(BF16)
    ct[1] = jnp.zeros((B, D), BF16)
    row = lax.broadcasted_iota(jnp.int32, (D, L), 1) % ROWS
    dim = lax.broadcasted_iota(jnp.int32, (D, L), 0)

    def query_documents(kb, _):
        doc = document(kb * B + c * 256 + y * ROWS + row) + ROWS
        other = (dim >= ROWS) & (dim < ROWS + 3) & (dim != doc)
        qd[kb] = jnp.where(dim == row, 1.0, jnp.where(other, -BIG, 0.0)).astype(BF16)
        return 0

    lax.fori_loop(0, SEQ // B, query_documents, 0)
    acc[0] = jnp.zeros((VR, L), jnp.float32)
    mref[...] = jnp.full_like(mref, -BIG)

    def prepare_queries(h):
        def turn_queries(xs, _):
            drain(qbuf.at[0, pl.ds(0, 2)], r_q.at[h, xs])
            for t in range(4):
                l, zz = 2 * xs + t // 2, t % 2
                tile = jnp.concatenate([qbuf[h, l, zz, :, j * D : (j + 1) * D] for j in range(SHARE)], axis=0)
                qs[h * 16 + 4 * xs + t] = tile.T
            return 0

        lax.fori_loop(0, 4, turn_queries, 0)

    def prepare(h):
        def turn_values(xs, _):
            for o in range(4):
                drain(whole, r_s.at[h, o, xs])
            for t in range(4):
                vt[4 * xs + t, 0:D, :] = kvs[h][4 * xs + t, :, :, 1].reshape(B, D).T
            return 0

        lax.fori_loop(0, 4, turn_values, 0)

    def work(h, zz, between):
        kv = kvs[h]

        def first_block(l):
            t0 = l * 1024 + (c + 2 * zz) * 256 + y * ROWS
            return jnp.where(t0 >= s2, s2, jnp.where(t0 >= s1, s1, 0)) // B

        def advance(l, kb):
            done = kb >= 2 * l + zz
            l2 = jnp.where(done, jnp.minimum(l + 1, 7), l)
            return l2, jnp.where(done, first_block(l2), kb + 1)

        def score(l, kb, par):
            mask = ct[jnp.where(kb == 2 * l + zz, 0, 1)]
            left = jnp.concatenate([kv[kb, :, :, 0].reshape(B, D), kd[kb] + mask], axis=1)
            right = jnp.concatenate([qs[h * 16 + 2 * l + zz], qd[2 * l + zz]], axis=0)
            s = jnp.dot(left, right, preferred_element_type=jnp.float32) * FACTOR
            sbuf[par] = s
            mc[par, 0:1, :] = jnp.max(s, axis=0, keepdims=True)

        def weigh(first, par):
            before = jnp.where(first == 1, -1e30, mref[0:1, :])
            top = jnp.maximum(before, mc[par, 0:1, :])
            mref[0:1, :] = top
            alr[par, 0:1, :] = jnp.exp2(before - top)
            pbuf[par] = jnp.exp2(sbuf[par] - top).astype(BF16)

        def collect(i, kb, par):
            pv = jnp.dot(vt[kb], pbuf[par], preferred_element_type=jnp.float32)
            acc[i + 1] = acc[i] * alr[par, 0:1, :] + pv

        def opens(l, kb):
            return (kb == first_block(l)).astype(jnp.int32)

        l0 = jnp.int32(0)
        b0 = first_block(l0)
        l1, b1 = advance(l0, b0)
        score(l0, b0, 0)
        score(l1, b1, 1)
        weigh(jnp.int32(1), 0)

        def two(j, carry):
            b0, b1, f1, l1 = carry
            for par in range(2):
                collect(2 * j + par, b0, par)
                weigh(f1, 1 - par)
                l2, b2 = advance(l1, b1)
                score(l2, b2, par)
                b0, b1, f1, l1 = b1, b2, opens(l2, b2), l2
            return b0, b1, f1, l1

        carry = (b0, b1, opens(l1, b1), l1)
        pairs = STEPS[zz] // 2
        if between is None:
            lax.fori_loop(0, pairs, two, carry)
        else:
            carry = lax.fori_loop(0, pairs // 2, two, carry)
            between(h + 1)
            lax.fori_loop(pairs // 2, pairs, two, carry)

        def count(l, done):
            done = done + 2 * l + zz - first_block(l) + 1
            last[l] = jnp.minimum(done, STEPS[zz])
            return done

        lax.fori_loop(0, 8, count, jnp.int32(0))
        to_z = c + 2 * zz
        cols = pl.ds(pl.multiple_of((z * 2 + h) * SHARE * D, 128), SHARE * D)

        def finish(j, _):
            l = (di + j) % 8
            i = last[l]
            a = acc[i, 0:D, :] / acc[i, D : D + 1, :]
            at = a.T.astype(BF16)
            tile = obuf.at[h, l, zz]
            for o in range(SHARE):
                obuf[h, l, zz, :, o * D : (o + 1) * D] = at[o * ROWS : (o + 1) * ROWS, :]
            own = (l == di) & (to_z == z)
            result = out_ref.at[0, x, :, cols]

            @pl.when(own)
            def _():
                pltpu.make_async_copy(tile, result, r_out).start()

            @pl.when(jnp.logical_not(own))
            def _():
                remote(tile, result, s_out.at[h, zz, l], r_out, (to_z * 4 + y, l))

            return 0

        lax.fori_loop(0, 8, finish, 0)

    forward(0)
    spread_head(1)
    relay(0)
    prepare_queries(0)
    complete(0)
    forward(1)
    prepare(0)
    work(0, 0, None)
    relay(1)
    work(0, 1, complete)
    prepare_queries(1)
    prepare(1)
    work(1, 0, None)
    work(1, 1, None)

    drain(out_ref, r_out)
    for h in range(2):
        for dx in range(4):
            if dx:
                drain(whole, s_kv.at[h, dx])
                drain(qbuf.at[0, pl.ds(0, 2)], s_q.at[h, dx])
            else:

                @pl.when(mine)
                def _():
                    drain(kva.at[0, 0, pl.ds(0, 3)], s_kv.at[h, dx])
                    drain(qbuf.at[0, pl.ds(0, 3), 0], s_q.at[h, dx])

                @pl.when(jnp.logical_not(mine))
                def _():
                    drain(whole, s_kv.at[h, dx])
                    drain(qbuf.at[0, pl.ds(0, 2)], s_q.at[h, dx])

    def sent(i, _):
        for h in range(2):
            for o in range(3):
                drain(whole, s_f.at[h, o, i])
            for o in range(5):
                drain(whole if o > 1 else part_of_one, s_r.at[h, o, i])
        return 0

    lax.fori_loop(0, 4, sent, 0)

    def returned(l, _):
        for h in range(2):
            for zz in range(2):

                @pl.when(jnp.logical_not((l == di) & (c + 2 * zz == z)))
                def _():
                    drain(obuf.at[0, 0, 0], s_out.at[h, zz, l])

        return 0

    lax.fori_loop(0, 8, returned, 0)


def per_device(query_rows, key_rows, value_rows, segment_ids):
    dma = pltpu.SemaphoreType.DMA
    vmem = pltpu.VMEM
    any_space = pl.BlockSpec(memory_space=pl.ANY)
    return pl.pallas_call(
        kernel,
        out_shape=jax.ShapeDtypeStruct((1, 4, ROWS, 4096), BF16),
        in_specs=[pl.BlockSpec(memory_space=vmem)] + [any_space] * 3,
        out_specs=any_space,
        scratch_shapes=[
            vmem((2, 8, 2, ROWS, SHARE * D), BF16),
            vmem((16, 2, 4, 2, ROWS, D), BF16),
            vmem((16, 2, 4, 2, ROWS, D), BF16),
            vmem((TILES, D, L), BF16),
            vmem((16, D, L), BF16),
            vmem((16, B, D), BF16),
            vmem((16, VR, B), BF16),
            vmem((2, B, D), BF16),
            vmem((2, B, L), jnp.float32),
            vmem((2, B, L), BF16),
            vmem((SLOTS, VR, L), jnp.float32),
            vmem((8, L), jnp.float32),
            vmem((2, 8, L), jnp.float32),
            vmem((2, 8, L), jnp.float32),
            vmem((2, 8, 2, ROWS, SHARE * D), BF16),
            pltpu.SMEM((8,), jnp.int32),
            dma((2, 4)), dma((2, 4)), dma((2, 4)), dma((2, 4)), dma((2, 3, 4)), dma((2, 2, 4)),
            dma((2, 5, 4)), dma((2, 2, 4)), dma((2, 4, 4)), dma((2, 2, 8)), dma(()),
        ],
        compiler_params=pltpu.CompilerParams(
            collective_id=0, has_side_effects=True, vmem_limit_bytes=60 * 2**20
        ),
    )(segment_ids, query_rows, key_rows, value_rows)


def solution(mesh):
    return jax.shard_map(
        per_device,
        mesh=mesh,
        in_specs=(
            P("dp", None, "grp", None),
            P("dp", None, "grp", None),
            P("dp", None, "grp", None),
            P(),
        ),
        out_specs=P("dp", None, "grp", None),
        check_vma=False,
    )
```

```python
import math

import jax
import jax.numpy as jnp
import numpy as np
from jax import lax
from jax.experimental import pallas as pl
from jax.experimental.pallas import tpu as pltpu
from jax.sharding import PartitionSpec as P

MESH = pl.DeviceIdType.MESH
SEQ = 8192
ROWS = 64
SHARE = 4
D = 128
L = SHARE * ROWS
TILES = 32
B = 512
VR = D + 16
BIG = float(2**20)
LONGEST = 5461
FACTOR = float(np.log2(np.e) / math.sqrt(D))
BF16 = jnp.bfloat16


def phase_steps():
    worst = [0] * 2
    cuts = np.arange(0, SEQ, ROWS) + 1
    s1, s2 = np.meshgrid(cuts, cuts, indexing="ij")
    slack = LONGEST + ROWS
    fits = (s2 >= s1) & (s1 <= slack) & (s2 - s1 <= slack) & (SEQ - s2 <= slack)
    s1, s2 = s1[fits], s2[fits]
    for zz in range(2):
        for c in range(2):
            for y in range(4):
                count = np.zeros(s1.shape, int)
                for l in range(8):
                    t0 = l * 1024 + (c + 2 * zz) * 256 + y * ROWS
                    start = np.where(t0 >= s2, s2, np.where(t0 >= s1, s1, 0))
                    count += t0 // B - start // B + 1
                worst[zz] = max(worst[zz], int(count.max()))
    return [n + n % 2 for n in worst]


STEPS = phase_steps()
SLOTS = max(STEPS) + 2


def drain(ref, sem):
    pltpu.make_async_copy(ref, ref, sem).wait()


def kernel(
    seg_ref, q_ref, k_ref, v_ref, out_ref, qbuf, kva, kvb, qs, qd, kd, vt, ct, sbuf, pbuf, acc, mref, mc, alr, obuf, last,
    s_kv, r_kv, s_q, r_q, s_f, r_f, s_r, r_r, r_s, s_out, r_out,
):
    gi, di = lax.axis_index("grp"), lax.axis_index("dp")
    x, y, z, c = di // 2, gi % 4, gi // 4, di % 2
    core = z % 2
    mine = core == c
    other_core = (gi, x * 2 + 1 - c)
    up, down, far = (y + 1) % 4, (y + 3) % 4, (y + 2) % 4
    up_chip, down_chip = (z * 4 + up, di), (z * 4 + down, di)
    kvs = (kva, kvb)

    barrier = pltpu.get_barrier_semaphore()
    n = 0
    for dx in range(4):
        for dz in range(4):
            for dc in range(2):
                if dx or dz or dc:
                    to = (((z + dz) % 4) * 4 + y, ((x + dx) % 4) * 2 + (c + dc) % 2)
                    pl.semaphore_signal(barrier, inc=1, device_id=to, device_id_type=MESH)
                    n += 1
    for to in (up_chip, down_chip):
        pl.semaphore_signal(barrier, inc=1, device_id=to, device_id_type=MESH)
        n += 1
    pl.semaphore_wait(barrier, n)

    def remote(src, dst, send, recv, to):
        pltpu.make_async_remote_copy(
            src_ref=src, dst_ref=dst, send_sem=send, recv_sem=recv, device_id=to, device_id_type=MESH
        ).start()

    def spread(pairs, h, width, send, recv):
        for dx in range(4):
            for dz in range(4):
                g, z2 = (x + dx) % 4, (z + dz) % 4
                cols = pl.ds(pl.multiple_of((z2 * 2 + h) * width, 128), width)
                to = (z2 * 4 + y, g * 2 + core)
                for src, dst in pairs:
                    piece = src.at[0, g, :, cols]
                    if dx or dz:
                        remote(piece, dst, send.at[h, dx], recv.at[h, x], to)
                    else:

                        @pl.when(mine)
                        def _():
                            pltpu.make_async_copy(piece, dst, recv.at[h, x]).start()

                        @pl.when(jnp.logical_not(mine))
                        def _():
                            remote(piece, dst, send.at[h, dx], recv.at[h, x], to)

    def spread_head(h):
        block = di * 2 + z // 2
        spread(((k_ref, kvs[h].at[block, core, y, 0]), (v_ref, kvs[h].at[block, core, y, 1])), h, D, s_kv, r_kv)
        spread(((q_ref, qbuf.at[h, di, z // 2]),), h, SHARE * D, s_q, r_q)

    whole, part_of_one = kva.at[0, 0], kva.at[0, 0, :, 0]

    def source(i):
        return (x + 4 - i) % 4

    def part(h, xs, whose):
        return kvs[h].at[pl.ds(4 * xs, 4), c, whose]

    def forward(h):
        for i in range(4):
            xs = source(i)
            drain(whole, r_kv.at[h, xs])
            own = part(h, xs, y)
            remote(own, own, s_f.at[h, 0, i], r_f.at[h, 0, xs], up_chip)
            remote(own, own, s_f.at[h, 1, i], r_f.at[h, 1, xs], down_chip)
            remote(own, own, s_f.at[h, 2, i], r_s.at[h, 0, xs], other_core)

    def relay(h):
        for i in range(4):
            xs = source(i)
            drain(whole, r_f.at[h, 0, xs])
            keys = kvs[h].at[pl.ds(4 * xs, 4), c, down, 0]
            remote(keys, keys, s_r.at[h, 0, i], r_r.at[h, 0, xs], up_chip)
            drain(whole, r_f.at[h, 1, xs])
            values = kvs[h].at[pl.ds(4 * xs, 4), c, up, 1]
            remote(values, values, s_r.at[h, 1, i], r_r.at[h, 1, xs], down_chip)
            remote(part(h, xs, down), part(h, xs, down), s_r.at[h, 2, i], r_s.at[h, 1, xs], other_core)
            remote(part(h, xs, up), part(h, xs, up), s_r.at[h, 3, i], r_s.at[h, 2, xs], other_core)

    def complete(h):
        for i in range(4):
            xs = source(i)
            drain(part_of_one, r_r.at[h, 0, xs])
            drain(part_of_one, r_r.at[h, 1, xs])
            remote(part(h, xs, far), part(h, xs, far), s_r.at[h, 4, i], r_s.at[h, 3, xs], other_core)

    spread_head(0)

    labels = seg_ref[pl.ds(x, 1), :]
    s1 = jnp.sum((labels == 0).astype(jnp.int32))
    s2 = s1 + jnp.sum((labels == 1).astype(jnp.int32))

    def document(pos):
        return jnp.where(pos >= s2, 2, jnp.where(pos >= s1, 1, 0))

    u = lax.broadcasted_iota(jnp.int32, (B, D), 0)
    r = lax.broadcasted_iota(jnp.int32, (B, D), 1)

    def key_documents(kb, _):
        kd[kb] = jnp.where(r == document(u + kb * B) + ROWS, 1.0, 0.0).astype(BF16)
        vt[kb, D:VR, :] = jnp.ones((VR - D, B), BF16)
        return 0

    lax.fori_loop(0, SEQ // B, key_documents, 0)
    ct[0] = jnp.where((r < ROWS) & (u > c * 256 + y * ROWS + r), -BIG, 0.0).astype(BF16)
    ct[1] = jnp.zeros((B, D), BF16)
    row = lax.broadcasted_iota(jnp.int32, (D, L), 1) % ROWS
    dim = lax.broadcasted_iota(jnp.int32, (D, L), 0)

    def query_documents(kb, _):
        doc = document(kb * B + c * 256 + y * ROWS + row) + ROWS
        other = (dim >= ROWS) & (dim < ROWS + 3) & (dim != doc)
        qd[kb] = jnp.where(dim == row, 1.0, jnp.where(other, -BIG, 0.0)).astype(BF16)
        return 0

    lax.fori_loop(0, SEQ // B, query_documents, 0)
    acc[0] = jnp.zeros((VR, L), jnp.float32)
    mref[...] = jnp.full_like(mref, -BIG)

    def prepare_queries(h):
        def turn_queries(xs, _):
            drain(qbuf.at[0, pl.ds(0, 2)], r_q.at[h, xs])
            for t in range(4):
                l, zz = 2 * xs + t // 2, t % 2
                tile = jnp.concatenate([qbuf[h, l, zz, :, j * D : (j + 1) * D] for j in range(SHARE)], axis=0)
                qs[h * 16 + 4 * xs + t] = tile.T
            return 0

        lax.fori_loop(0, 4, turn_queries, 0)

    def prepare(h):
        def turn_values(xs, _):
            for o in range(4):
                drain(whole, r_s.at[h, o, xs])
            for t in range(4):
                vt[4 * xs + t, 0:D, :] = kvs[h][4 * xs + t, :, :, 1].reshape(B, D).T
            return 0

        lax.fori_loop(0, 4, turn_values, 0)

    def work(h, zz, between):
        kv = kvs[h]

        def first_block(l):
            t0 = l * 1024 + (c + 2 * zz) * 256 + y * ROWS
            return jnp.where(t0 >= s2, s2, jnp.where(t0 >= s1, s1, 0)) // B

        def advance(l, kb):
            done = kb >= 2 * l + zz
            l2 = jnp.where(done, jnp.minimum(l + 1, 7), l)
            return l2, jnp.where(done, first_block(l2), kb + 1)

        def score(l, kb, par):
            mask = ct[jnp.where(kb == 2 * l + zz, 0, 1)]
            left = jnp.concatenate([kv[kb, :, :, 0].reshape(B, D), kd[kb] + mask], axis=1)
            right = jnp.concatenate([qs[h * 16 + 2 * l + zz], qd[2 * l + zz]], axis=0)
            s = jnp.dot(left, right, preferred_element_type=jnp.float32) * FACTOR
            sbuf[par] = s
            mc[par, 0:1, :] = jnp.max(s, axis=0, keepdims=True)

        def weigh(first, par):
            before = jnp.where(first == 1, -1e30, mref[0:1, :])
            top = jnp.maximum(before, mc[par, 0:1, :])
            mref[0:1, :] = top
            alr[par, 0:1, :] = jnp.exp2(before - top)
            pbuf[par] = jnp.exp2(sbuf[par] - top).astype(BF16)

        def collect(i, kb, par):
            pv = jnp.dot(vt[kb], pbuf[par], preferred_element_type=jnp.float32)
            acc[i + 1] = acc[i] * alr[par, 0:1, :] + pv

        def opens(l, kb):
            return (kb == first_block(l)).astype(jnp.int32)

        l0 = jnp.int32(0)
        b0 = first_block(l0)
        l1, b1 = advance(l0, b0)
        score(l0, b0, 0)
        score(l1, b1, 1)
        weigh(jnp.int32(1), 0)

        def two(j, carry):
            b0, b1, f1, l1 = carry
            for par in range(2):
                collect(2 * j + par, b0, par)
                weigh(f1, 1 - par)
                l2, b2 = advance(l1, b1)
                score(l2, b2, par)
                b0, b1, f1, l1 = b1, b2, opens(l2, b2), l2
            return b0, b1, f1, l1

        carry = (b0, b1, opens(l1, b1), l1)
        pairs = STEPS[zz] // 2
        if between is None:
            lax.fori_loop(0, pairs, two, carry)
        else:
            carry = lax.fori_loop(0, pairs // 2, two, carry)
            between(h + 1)
            lax.fori_loop(pairs // 2, pairs, two, carry)

        def count(l, done):
            done = done + 2 * l + zz - first_block(l) + 1
            last[l] = jnp.minimum(done, STEPS[zz])
            return done

        lax.fori_loop(0, 8, count, jnp.int32(0))
        to_z = c + 2 * zz
        cols = pl.ds(pl.multiple_of((z * 2 + h) * SHARE * D, 128), SHARE * D)

        def finish(j, _):
            l = (di + j) % 8
            i = last[l]
            a = acc[i, 0:D, :] / acc[i, D : D + 1, :]
            at = a.T.astype(BF16)
            tile = obuf.at[h, l, zz]
            for o in range(SHARE):
                obuf[h, l, zz, :, o * D : (o + 1) * D] = at[o * ROWS : (o + 1) * ROWS, :]
            own = (l == di) & (to_z == z)
            result = out_ref.at[0, x, :, cols]

            @pl.when(own)
            def _():
                pltpu.make_async_copy(tile, result, r_out).start()

            @pl.when(jnp.logical_not(own))
            def _():
                remote(tile, result, s_out.at[h, zz, l], r_out, (to_z * 4 + y, l))

            return 0

        lax.fori_loop(0, 8, finish, 0)

    forward(0)
    spread_head(1)
    relay(0)
    prepare_queries(0)
    complete(0)
    forward(1)
    prepare(0)
    work(0, 0, None)
    relay(1)
    work(0, 1, complete)
    prepare_queries(1)
    prepare(1)
    work(1, 0, None)
    work(1, 1, None)

    for h in range(2):
        for dx in range(4):
            if dx:
                drain(whole, s_kv.at[h, dx])
                drain(qbuf.at[0, pl.ds(0, 2)], s_q.at[h, dx])
            else:

                @pl.when(mine)
                def _():
                    drain(kva.at[0, 0, pl.ds(0, 3)], s_kv.at[h, dx])
                    drain(qbuf.at[0, pl.ds(0, 3), 0], s_q.at[h, dx])

                @pl.when(jnp.logical_not(mine))
                def _():
                    drain(whole, s_kv.at[h, dx])
                    drain(qbuf.at[0, pl.ds(0, 2)], s_q.at[h, dx])

    def sent(i, _):
        for h in range(2):
            for o in range(3):
                drain(whole, s_f.at[h, o, i])
            for o in range(5):
                drain(whole if o > 1 else part_of_one, s_r.at[h, o, i])
        return 0

    lax.fori_loop(0, 4, sent, 0)

    def returned(l, _):
        for h in range(2):
            for zz in range(2):

                @pl.when(jnp.logical_not((l == di) & (c + 2 * zz == z)))
                def _():
                    drain(obuf.at[0, 0, 0], s_out.at[h, zz, l])

        return 0

    lax.fori_loop(0, 8, returned, 0)
    drain(out_ref, r_out)


def per_device(query_rows, key_rows, value_rows, segment_ids):
    dma = pltpu.SemaphoreType.DMA
    vmem = pltpu.VMEM
    any_space = pl.BlockSpec(memory_space=pl.ANY)
    return pl.pallas_call(
        kernel,
        out_shape=jax.ShapeDtypeStruct((1, 4, ROWS, 4096), BF16),
        in_specs=[pl.BlockSpec(memory_space=vmem)] + [any_space] * 3,
        out_specs=any_space,
        scratch_shapes=[
            vmem((2, 8, 2, ROWS, SHARE * D), BF16),
            vmem((16, 2, 4, 2, ROWS, D), BF16),
            vmem((16, 2, 4, 2, ROWS, D), BF16),
            vmem((TILES, D, L), BF16),
            vmem((16, D, L), BF16),
            vmem((16, B, D), BF16),
            vmem((16, VR, B), BF16),
            vmem((2, B, D), BF16),
            vmem((2, B, L), jnp.float32),
            vmem((2, B, L), BF16),
            vmem((SLOTS, VR, L), jnp.float32),
            vmem((8, L), jnp.float32),
            vmem((2, 8, L), jnp.float32),
            vmem((2, 8, L), jnp.float32),
            vmem((2, 8, 2, ROWS, SHARE * D), BF16),
            pltpu.SMEM((8,), jnp.int32),
            dma((2, 4)), dma((2, 4)), dma((2, 4)), dma((2, 4)), dma((2, 3, 4)), dma((2, 2, 4)),
            dma((2, 5, 4)), dma((2, 2, 4)), dma((2, 4, 4)), dma((2, 2, 8)), dma(()),
        ],
        compiler_params=pltpu.CompilerParams(
            collective_id=0, has_side_effects=True, vmem_limit_bytes=60 * 2**20
        ),
    )(segment_ids, query_rows, key_rows, value_rows)


def solution(mesh):
    return jax.shard_map(
        per_device,
        mesh=mesh,
        in_specs=(
            P("dp", None, "grp", None),
            P("dp", None, "grp", None),
            P("dp", None, "grp", None),
            P(),
        ),
        out_specs=P("dp", None, "grp", None),
        check_vma=False,
    )
```
